32 devices in a mesh: grp: 2 (over y), dev: 16 (over z, x, core).
Axes of the slice: x: 2, y: 2, z: 4, core: 2. Of those that a mesh axis runs over, the one named last changes fastest.
Arguments:
- valence_orbitals: bfloat16 [4, 48, 2304], replicated, may hold values from -6 to 6
- conduction_orbitals: bfloat16 [64, 48, 2304], P('dev'), may hold values from -6 to 6
- valence_energy: float32 [4], replicated, may hold values from -6 to -1
- conduction_energy: float32 [64], P('dev'), may hold values from 0.5 to 6
- pair_index: int32 [16, 8], P('dev', 'grp'), may hold values from 0 to 15, as said below
- grid_map: int32 [24576], replicated, may hold values from 0 to 110591, as said below
Outputs:
- response: float32 [24576, 12288], P('dev', 'grp')
The draws below stay inside these ranges and needn't reach their ends.
Inputs may be any that keep to these rules, and one draw needn't show every extreme that they name: `pair_index`: each row holds 8 distinct numbers. `grid_map`: all entries distinct.
All inputs are finite; a program needn't handle non-finite values.
Results may differ from the reference program's by a relative error of at most 0.004.
Values may be sent and summed in bfloat16 or wider, within the bound.
No kernel may reach another device: no remote copies, remote signals or barrier semaphores. Data moves between devices by JAX's collectives and lax.ppermute only.
A program may use at most 192 MiB of HBM per device.

```python
import math
import jax
import jax.numpy as jnp
from jax import lax

NV = 4
CB_DEV = 4
SEL = 8
NCOND = 64
NTRANS = 128
NR1 = 48
NR2 = 48
NR3 = 48
NG = 24576
NGC = 12288
N_DEV = 16


def draw_pair_index(key, part):
    key = jax.random.fold_in(key, 11)
    row_keys = jax.random.split(key, NCOND // CB_DEV)

    def one_row(row_key):
        return jax.random.permutation(row_key, NV * CB_DEV)[:SEL]
    return jax.vmap(one_row)(row_keys).astype(jnp.int32)


def draw_grid_map(key, part):
    key = jax.random.fold_in(key, 23)
    first_key, second_key = jax.random.split(key)
    points = NR1 * NR2 * NR3
    inner = jax.random.permutation(first_key, points - 2)[:NG - 2] + 1
    ends = jnp.array([0, points - 1], dtype=jnp.int32)
    joined = jnp.concatenate([ends, inner.astype(jnp.int32)])
    return jax.random.permutation(second_key, joined).astype(jnp.int32)


def block_scale(own_key, dims, cuts, least, top_value):
    factor_of = 1.0
    for position, shards_of in cuts:
        steps = jax.random.uniform(jax.random.fold_in(jax.random.fold_in(own_key, 6), position), (shards_of,), jnp.float32, least / len(cuts), top_value / len(cuts))
        factor_of = factor_of * jnp.repeat(jnp.exp(steps), dims[position] // shards_of).reshape((-1,) + (1,) * (len(dims) - 1 - position))
    return factor_of


def gaussian(key, shape, deviation, limit, cuts=(), kind=jnp.bfloat16):
    factor_of = block_scale(key, shape, cuts, -0.22, 0.18) if cuts else 1.0
    values = jax.random.normal(key, shape, jnp.float32) * deviation * factor_of
    return jnp.minimum(jnp.maximum(values, -limit), limit).astype(kind)


def setup_inputs(seed: int = 0) -> dict:
    arg_keys = jax.random.split(jax.random.key(seed), 7)
    valence_orbitals = gaussian(arg_keys[0], (NV, NR1, NR2 * NR3), 1.0, 6.0)
    conduction_orbitals = gaussian(arg_keys[1], (NCOND, NR1, NR2 * NR3), 1.0, 6.0, ((0, 16),))
    valence_energy = jnp.clip(jax.random.uniform(arg_keys[2], (NV,), jnp.float32, -6.0, -1.0), -6.0, -1.0)
    conduction_energy = jnp.clip(0.5 + 5.5 * jax.random.uniform(arg_keys[3], (NCOND,), jnp.float32) ** block_scale(arg_keys[3], (NCOND,), ((0, 16),), -0.2, 0.2), 0.5, 6.0)
    pair_index = draw_pair_index(jax.random.fold_in(arg_keys[6], 71), 0)
    grid_map = draw_grid_map(jax.random.fold_in(arg_keys[6], 71), 0)
    return {"valence_orbitals": valence_orbitals, "conduction_orbitals": conduction_orbitals, "valence_energy": valence_energy, "conduction_energy": conduction_energy, "pair_index": pair_index, "grid_map": grid_map}


def pair_field(valence_orbitals, conduction_orbitals, valence_energy, conduction_energy, grid_map, valence_band, conduction_band):
    left = lax.dynamic_index_in_dim(valence_orbitals, valence_band, 0, keepdims=False).astype(jnp.float32)
    right = lax.dynamic_index_in_dim(conduction_orbitals, conduction_band, 0, keepdims=False).astype(jnp.float32)
    density = (left * right).reshape(NR1, NR2, NR3)
    spectrum = jnp.fft.fftn(density).reshape(-1)
    values = spectrum[grid_map]
    energy_gap = conduction_energy[conduction_band] - valence_energy[valence_band]
    factor = jnp.sqrt(4.0 / energy_gap) * (1.0 / math.sqrt(NR1 * NR2 * NR3))
    return jnp.stack([jnp.real(values) * factor, jnp.imag(values) * factor]).astype(jnp.bfloat16)

def reference(valence_orbitals, conduction_orbitals, valence_energy, conduction_energy, pair_index, grid_map):
    device_rows = jnp.arange(N_DEV, dtype=jnp.int32)[:, None]
    valence_bands = (pair_index // CB_DEV).astype(jnp.int32).reshape(-1)
    conduction_bands = (device_rows * CB_DEV + pair_index % CB_DEV).astype(jnp.int32).reshape(-1)

    def one_pair(bands):
        return pair_field(valence_orbitals, conduction_orbitals, valence_energy, conduction_energy, grid_map, bands[0], bands[1])
    pair_fields = lax.map(one_pair, (valence_bands, conduction_bands))
    flat = pair_fields.reshape(2 * NTRANS, NG).astype(jnp.float32)
    summed = jnp.dot(flat.T, flat[:, :NGC], preferred_element_type=jnp.float32)
    return -summed / math.sqrt(NTRANS)
```

```python
import math

import jax
import jax.numpy as jnp
import numpy as np
from jax import lax
from jax.experimental import pallas as pl
from jax.experimental.pallas import tpu as pltpu
from jax.sharding import PartitionSpec as P

NR1 = 48
NR2 = 48
NR3 = 48
NGC = 12288
HALF = NR3 // 2 + 1
FOLD = NR2 * NR3 // 2
LANES = 128
PER_PARITY = -(-(NR2 // 2 * HALF) // LANES) * LANES
COLUMNS = 2 * PER_PARITY
TILES = COLUMNS // LANES
VMEM = 60 * 1024 * 1024


def split_bf16(values):
    high = values.astype(jnp.bfloat16)
    low = (values - high.astype(values.dtype)).astype(jnp.bfloat16)
    return high, low


def plane_tables():
    r2 = np.arange(NR2 // 2)[:, None]
    r3 = np.arange(NR3)[None, :]
    table = np.zeros((2, FOLD, PER_PARITY, 2))
    for parity in range(2):
        for half_k2 in range(NR2 // 2):
            k2 = 2 * half_k2 + parity
            for k3 in range(HALF):
                angle = 2 * np.pi * ((k2 * r2 * NR3 + k3 * r3 * NR2) % (NR2 * NR3)) / (NR2 * NR3)
                table[parity, :, half_k2 * HALF + k3, 0] = np.cos(angle).reshape(-1)
                table[parity, :, half_k2 * HALF + k3, 1] = np.sin(angle).reshape(-1)
    table = table.reshape(2, FOLD, PER_PARITY // LANES, LANES, 2).transpose(0, 2, 1, 4, 3)
    table = table.reshape(TILES, FOLD, 2 * LANES).astype(np.float32)
    high = table.astype(jnp.bfloat16)
    low = (table - high.astype(np.float32)).astype(jnp.bfloat16)
    return high, low


def first_tables():
    counter = np.arange(NR1)
    angle = 2 * np.pi * (counter[:, None] * counter[None, :] % NR1) / NR1
    cosine, sine = np.cos(angle), np.sin(angle)
    table = np.block([[cosine, -sine], [-sine, -cosine]]).astype(np.float32)
    high = table.astype(jnp.bfloat16)
    low = (table - high.astype(np.float32)).astype(jnp.bfloat16)
    return high, low


def dot32(left, right):
    return jnp.dot(left, right, preferred_element_type=jnp.float32)


def spectrum_kernel(
    pairs, bands, valence_energy, conduction_energy, valence, conduction,
    plane_high, plane_low, first_high, first_low, table, folded_high, folded_low,
):
    step = pl.program_id(0)

    @pl.when(step == 0)
    def _():
        for pair in range(pairs):
            left = valence[bands[0, pair]].astype(jnp.float32)
            right = conduction[bands[1, pair]].astype(jnp.float32)
            density = left * right
            for parity in range(2):
                if parity == 0:
                    folded = density[:, :FOLD] + density[:, FOLD:]
                else:
                    folded = density[:, :FOLD] - density[:, FOLD:]
                high, low = split_bf16(folded)
                folded_high[parity, pair * NR1 : (pair + 1) * NR1, :] = high
                folded_low[parity, pair * NR1 : (pair + 1) * NR1, :] = low

    parity = step // (TILES // 2)
    high = folded_high[parity]
    plane = dot32(high, plane_high[0]) + (
        dot32(folded_low[parity], plane_high[0]) + dot32(high, plane_low[0])
    )
    stacked = jnp.concatenate(
        [
            jnp.concatenate(
                [
                    plane[pair * NR1 : (pair + 1) * NR1, :LANES],
                    plane[pair * NR1 : (pair + 1) * NR1, LANES:],
                ],
                axis=0,
            )
            for pair in range(pairs)
        ],
        axis=1,
    )
    high, low = split_bf16(stacked)
    spectra = dot32(first_high[...], high) + (
        dot32(first_low[...], high) + dot32(first_high[...], low)
    )
    inverse_root = 1.0 / math.sqrt(NR1 * NR2 * NR3)
    for pair in range(pairs):
        gap = conduction_energy[bands[1, pair]] - valence_energy[bands[0, pair]]
        factor = jnp.sqrt(4.0 / jnp.full((8, LANES), gap, jnp.float32)) * inverse_root
        block = spectra[:, pair * LANES : (pair + 1) * LANES]
        block = block * factor[0:1, :]
        table[pair * 2 * NR1 : (pair + 1) * 2 * NR1, :] = block.astype(jnp.bfloat16)


def whole(array):
    return pl.BlockSpec(array.shape, lambda *_: (0,) * array.ndim)


def spectra_table(valence, conduction, valence_energy, conduction_energy, bands):
    pairs = bands.shape[1]
    plane_high, plane_low = plane_tables()
    first_high, first_low = first_tables()
    scalars = pl.BlockSpec(memory_space=pltpu.SMEM)
    tile = pl.BlockSpec((1, FOLD, 2 * LANES), lambda i: (i, 0, 0))

    def kernel(*refs):
        spectrum_kernel(pairs, *refs)

    return pl.pallas_call(
        kernel,
        grid=(TILES,),
        in_specs=[scalars, scalars, scalars, whole(valence), whole(conduction), tile, tile]
        + [whole(first_high), whole(first_low)],
        out_specs=pl.BlockSpec((pairs * 2 * NR1, LANES), lambda i: (0, i)),
        out_shape=jax.ShapeDtypeStruct((pairs * 2 * NR1, COLUMNS), jnp.bfloat16),
        scratch_shapes=[
            pltpu.VMEM((2, pairs * NR1, FOLD), jnp.bfloat16),
            pltpu.VMEM((2, pairs * NR1, FOLD), jnp.bfloat16),
        ],
        compiler_params=pltpu.CompilerParams(vmem_limit_bytes=VMEM),
        name="spectra",
    )(
        bands, valence_energy, conduction_energy, valence, conduction,
        jnp.asarray(plane_high), jnp.asarray(plane_low), jnp.asarray(first_high), jnp.asarray(first_low),
    )


DEPTH = 256


def plane_codes(point):
    first = point // (NR2 * NR3)
    second = point // NR3 % NR2
    third = point % NR3
    mirrored = third >= HALF
    first = jnp.where(mirrored, (NR1 - first) % NR1, first)
    second = jnp.where(mirrored, (NR2 - second) % NR2, second)
    third = jnp.where(mirrored, NR3 - third, third)
    column = second % 2 * PER_PARITY + second // 2 * HALF + third
    sign = jnp.where(mirrored, -1.0, 1.0)
    return column, first, sign


def pick_strip(point, table):
    width = point.shape[1]
    column, first, sign = plane_codes(point)
    counter = lax.broadcasted_iota(jnp.int32, (DEPTH, width), 0)
    counter = counter.astype(jnp.float32).astype(jnp.bfloat16)
    total = None
    for part in range(COLUMNS // DEPTH):
        wanted = (column - part * DEPTH).astype(jnp.float32).astype(jnp.bfloat16)
        hot = jnp.where(counter == wanted, jnp.bfloat16(1), jnp.bfloat16(0))
        term = dot32(table[:, part * DEPTH : (part + 1) * DEPTH], hot)
        total = term if total is None else total + term
    chosen = lax.broadcasted_iota(jnp.int32, (NR1, width), 0) == first
    rows = []
    for field in range(table.shape[0] // NR1):
        block = jnp.where(chosen, total[field * NR1 : (field + 1) * NR1, :], 0.0)
        row = jnp.sum(block, axis=0, keepdims=True)
        rows.append(row * sign if field % 2 else row)
    return jnp.concatenate(rows, axis=0).astype(jnp.bfloat16)


def pick(strips, table, turn, where, count):
    width = strips.shape[3]
    fields = table.shape[0] // NR1

    def kernel(_, points, table, picked):
        picked[...] = pick_strip(points[0, 0], table)

    grid_spec = pltpu.PrefetchScalarGridSpec(
        num_scalar_prefetch=1,
        grid=(count,),
        in_specs=[
            pl.BlockSpec((1, 1, 1, width), lambda i, at: (at[0] * count + i, turn, 0, 0)),
            pl.BlockSpec(memory_space=pltpu.VMEM),
        ],
        out_specs=pl.BlockSpec((fields, width), lambda i, at: (0, i)),
    )
    return pl.pallas_call(
        kernel,
        grid_spec=grid_spec,
        out_shape=jax.ShapeDtypeStruct((fields, count * width), jnp.bfloat16),
        compiler_params=pltpu.CompilerParams(vmem_limit_bytes=VMEM // 3),
        cost_estimate=pl.CostEstimate(
            flops=2 * table.size * count * width, bytes_accessed=table.size * 2, transcendentals=0
        ),
        name="pick",
    )(jnp.full((1,), where, jnp.int32), strips, table)


def response_kernel(pieces, rounds, scale, place, rows, *refs):
    out, left, right = refs[-3:]

    @pl.when(pl.program_id(0) == 0)
    def _():
        left[...] = rows[...].T

    for turn in range(rounds):
        blocks = refs[turn * len(pieces) : (turn + 1) * len(pieces)]

        @pl.when(pl.program_id(0) % rounds == turn)
        def _():
            for offsets, block in zip(pieces, blocks):
                size = block.shape[0] // len(offsets)
                for position, offset in enumerate(offsets):
                    start = pl.multiple_of(jnp.bitwise_xor(place[0], offset) * size, size)
                    right[pl.ds(start, size), :] = block[position * size : (position + 1) * size, :]

    out[...] = dot32(left[...], right[...]) * scale


def response(out, shape, row_block, place, rows, pieces, blocks, scale, width):
    depth, count = rows.shape
    rounds = len(blocks)

    def kernel(*refs):
        response_kernel(pieces, rounds, scale, *refs)

    operands = [place, rows]
    in_specs = [pl.BlockSpec(memory_space=pltpu.SMEM), whole(rows)]
    for held in blocks:
        operands += held
        in_specs += [pl.BlockSpec((block.shape[0], width), lambda i: (0, i // rounds)) for block in held]
    aliases = {}
    if out is not None:
        aliases = {len(operands): 0}
        operands.append(out)
        in_specs.append(pl.BlockSpec(memory_space=pl.ANY))
    return pl.pallas_call(
        kernel,
        grid=(shape[1] // width,),
        in_specs=in_specs,
        out_specs=pl.BlockSpec((count, width), lambda i: (row_block, i)),
        out_shape=jax.ShapeDtypeStruct(shape, jnp.float32),
        scratch_shapes=[
            pltpu.VMEM((count, depth), jnp.bfloat16),
            pltpu.VMEM((depth, width), jnp.bfloat16),
        ],
        input_output_aliases=aliases,
        compiler_params=pltpu.CompilerParams(vmem_limit_bytes=VMEM // 3),
        cost_estimate=pl.CostEstimate(
            flops=2 * depth * count * shape[1], bytes_accessed=4 * count * shape[1], transcendentals=0
        ),
        name="response",
    )(*operands)


def after(values, *others):
    return lax.optimization_barrier((values, others))[0]


def any_mesh(groups, size, table, grid_map, depth, scale):
    zero = jnp.zeros((1,), jnp.int32)
    width = 1024
    strips = grid_map.reshape(-1, 1, 1, width)
    everything = pick(strips, table, 0, 0, strips.shape[0])
    fields = everything.shape[0]
    block = lax.all_to_all(everything[:, :NGC], "grp", split_axis=1, concat_axis=0, tiled=True)
    blocks = lax.all_gather(block, "dev", axis=0, tiled=True)
    here = lax.all_to_all(everything, "dev", split_axis=1, concat_axis=0, tiled=True)
    rows = lax.all_gather(here, "grp", axis=0).reshape(groups, size, fields, -1)
    rows = rows.transpose(1, 0, 2, 3).reshape(depth, -1)
    shape = (rows.shape[1], NGC // groups)
    return response(None, shape, 0, zero, rows, [tuple(range(size))], [[blocks]], scale, 512)


def per_device(
    groups, size, valence_orbitals, conduction_orbitals, valence_energy, conduction_energy, pair_index, grid_map
):
    bands_here = conduction_orbitals.shape[0]
    own_rows = grid_map.shape[0] // size
    pair_numbers = pair_index.reshape(-1)
    fields = 2 * pair_numbers.shape[0]
    depth = groups * size * fields
    scale = -1.0 / math.sqrt(depth // 2)
    bands = jnp.stack([pair_numbers // bands_here, pair_numbers % bands_here])
    table = spectra_table(
        valence_orbitals, conduction_orbitals, valence_energy, conduction_energy, bands
    )
    if groups != 2 or size != 16:
        return any_mesh(groups, size, table, grid_map, depth, scale)

    me = lax.axis_index("grp")
    place = jnp.full((1,), lax.axis_index("dev"), jnp.int32)
    strips = grid_map.reshape(size, 2, 1, own_rows // 2)

    def across(values):
        return lax.ppermute(values, "grp", [(0, 1), (1, 0)])

    def swap(values, bit):
        return lax.ppermute(values, "dev", [(i, i ^ bit) for i in range(size)])

    def stack(*values):
        return jnp.concatenate(values, axis=0)

    def quarter(turn, where, *others):
        return pick(strips, after(table, *others), turn, where, size // 4)

    def to_rows(low, high):
        whole_round = jnp.concatenate(
            [jnp.where(me == 0, low[0], low[1]), jnp.where(me == 0, low[1], low[0]), *high], axis=1
        )
        return lax.all_to_all(whole_round, "dev", split_axis=1, concat_axis=0, tiled=True)

    def both_groups(here, there):
        both = jnp.stack([here.reshape(size, fields, -1), there.reshape(size, fields, -1)], axis=1)
        return both.reshape(depth, -1)

    other0 = quarter(0, 1 - me)
    sent0 = across(other0)
    mine0 = quarter(0, me, other0)
    own0 = stack(mine0, sent0)
    far0 = swap(own0, 8)
    other1 = quarter(1, 1 - me, own0)
    sent1 = across(other1)
    mine1 = quarter(1, me, other1)
    own1 = stack(mine1, sent1)
    near0 = stack(own0, far0)
    far1 = swap(own1, 8)
    side0, next0 = swap(near0, 2), swap(near0, 4)
    high0 = [quarter(0, 2, mine1, near0, own1)]
    high0.append(quarter(0, 3, *high0))
    near1 = stack(own1, far1)
    corner0 = swap(next0, 2)
    side1, next1 = swap(near1, 2), swap(near1, 4)
    here0 = to_rows([mine0, other0], high0)
    high1 = [quarter(1, 2, *high0, side0, next0, near1)]
    high1.append(quarter(1, 3, *high1, here0))
    there0 = across(here0)
    corner1 = swap(next1, 2)
    here1 = to_rows([mine1, other1], high1)
    there1 = across(here1)
    blocks = [[near0, side0, next0, corner0], [near1, side1, next1, corner1]]
    blocks = [held + [swap(block, 1) for block in held] for held in blocks]
    pieces = [(0, 8), (2, 10), (4, 12), (6, 14)]
    pieces += [tuple(offset + 1 for offset in piece) for piece in pieces]

    shape = (own_rows, NGC // groups)
    width = own_rows // 2
    out = response(None, shape, 0, place, both_groups(here0, there0), pieces, blocks, scale, width)
    return response(out, shape, 1, place, both_groups(here1, there1), pieces, blocks, scale, width)


def solution(mesh):
    groups, size = mesh.shape["grp"], mesh.shape["dev"]

    def body(*args):
        return per_device(groups, size, *args)

    in_specs = (P(), P("dev", None, None), P(), P("dev"), P("dev", "grp"), P())
    out_specs = P("dev", "grp")
    return jax.shard_map(body, mesh=mesh, in_specs=in_specs, out_specs=out_specs, check_vma=False)
```

```python
import math

import jax
import jax.numpy as jnp
import numpy as np
from jax import lax
from jax.experimental import pallas as pl
from jax.experimental.pallas import tpu as pltpu
from jax.sharding import PartitionSpec as P

NR1 = 48
NR2 = 48
NR3 = 48
NGC = 12288
HALF = NR3 // 2 + 1
FOLD = NR2 * NR3 // 2
LANES = 128
PER_PARITY = -(-(NR2 // 2 * HALF) // LANES) * LANES
COLUMNS = 2 * PER_PARITY
VMEM = 60 * 1024 * 1024
SPECTRA_VMEM = 60 * 1024 * 1024


def split_bf16(values):
    high = values.astype(jnp.bfloat16)
    low = (values - high.astype(values.dtype)).astype(jnp.bfloat16)
    return high, low


def plane_tables():
    r2 = np.arange(NR2 // 2)[:, None]
    r3 = np.arange(NR3)[None, :]
    table = np.zeros((2, FOLD, PER_PARITY, 2))
    for parity in range(2):
        for half_k2 in range(NR2 // 2):
            k2 = 2 * half_k2 + parity
            for k3 in range(HALF):
                angle = 2 * np.pi * ((k2 * r2 * NR3 + k3 * r3 * NR2) % (NR2 * NR3)) / (NR2 * NR3)
                table[parity, :, half_k2 * HALF + k3, 0] = np.cos(angle).reshape(-1)
                table[parity, :, half_k2 * HALF + k3, 1] = np.sin(angle).reshape(-1)
    table = table.transpose(0, 1, 3, 2).reshape(2, FOLD, 2 * PER_PARITY).astype(np.float32)
    high = table.astype(jnp.bfloat16)
    low = (table - high.astype(np.float32)).astype(jnp.bfloat16)
    return high, low


def first_tables():
    counter = np.arange(NR1)
    angle = 2 * np.pi * (counter[:, None] * counter[None, :] % NR1) / NR1
    cosine, sine = np.cos(angle), np.sin(angle)
    table = np.block([[cosine, -sine], [-sine, -cosine]]).astype(np.float32)
    high = table.astype(jnp.bfloat16)
    low = (table - high.astype(np.float32)).astype(jnp.bfloat16)
    return np.concatenate([high, low])


def dot32(left, right):
    return jnp.dot(left, right, preferred_element_type=jnp.float32)


def three_products(high_low, right_high, right_low):
    half = high_low.shape[0] // 2
    both = dot32(high_low, right_high)
    return both[:half] + (both[half:] + dot32(high_low[:half], right_low))


def spectrum_kernel(
    pairs, chosen, valence_energy, conduction_energy, valence, conduction,
    plane_high, plane_low, first, table, folded,
):
    step = pl.program_id(0)
    rows = pairs * NR1
    bands_here = conduction.shape[0]

    @pl.when(step == 0)
    def _():
        for pair in range(pairs):
            left = valence[chosen[0, pair] // bands_here].astype(jnp.float32)
            right = conduction[chosen[0, pair] % bands_here].astype(jnp.float32)
            density = left * right
            for parity in range(2):
                if parity == 0:
                    values = density[:, :FOLD] + density[:, FOLD:]
                else:
                    values = density[:, :FOLD] - density[:, FOLD:]
                high, low = split_bf16(values)
                folded[parity, pair * NR1 : (pair + 1) * NR1, :] = high
                folded[parity, rows + pair * NR1 : rows + (pair + 1) * NR1, :] = low

    plane = three_products(folded[step], plane_high[0], plane_low[0])
    stacked = jnp.concatenate(
        [
            jnp.concatenate(
                [
                    plane[pair * NR1 : (pair + 1) * NR1, :PER_PARITY],
                    plane[pair * NR1 : (pair + 1) * NR1, PER_PARITY:],
                ],
                axis=0,
            )
            for pair in range(pairs)
        ],
        axis=1,
    )
    spectra = three_products(first[...], *split_bf16(stacked))
    inverse_root = 1.0 / math.sqrt(NR1 * NR2 * NR3)
    for pair in range(pairs):
        gap = conduction_energy[chosen[0, pair] % bands_here] - valence_energy[chosen[0, pair] // bands_here]
        factor = jnp.sqrt(4.0 / jnp.full((8, LANES), gap, jnp.float32)) * inverse_root
        block = spectra[:, pair * PER_PARITY : (pair + 1) * PER_PARITY]
        block = block * factor[0:1, 0:1]
        table[pair * 2 * NR1 : (pair + 1) * 2 * NR1, :] = block.astype(jnp.bfloat16)


def whole(array):
    return pl.BlockSpec(array.shape, lambda *_: (0,) * array.ndim)


def spectra_table(valence, conduction, valence_energy, conduction_energy, chosen):
    pairs = chosen.shape[1]
    plane_high, plane_low = plane_tables()
    first = first_tables()
    scalars = pl.BlockSpec(memory_space=pltpu.SMEM)
    tile = pl.BlockSpec((1, FOLD, 2 * PER_PARITY), lambda i: (i, 0, 0))

    def kernel(*refs):
        spectrum_kernel(pairs, *refs)

    return pl.pallas_call(
        kernel,
        grid=(2,),
        in_specs=[scalars, scalars, scalars, whole(valence), whole(conduction), tile, tile]
        + [whole(first)],
        out_specs=pl.BlockSpec((pairs * 2 * NR1, PER_PARITY), lambda i: (0, i)),
        out_shape=jax.ShapeDtypeStruct((pairs * 2 * NR1, COLUMNS), jnp.bfloat16),
        scratch_shapes=[
            pltpu.VMEM((2, 2 * pairs * NR1, FOLD), jnp.bfloat16),
        ],
        compiler_params=pltpu.CompilerParams(vmem_limit_bytes=SPECTRA_VMEM),
        name="spectra",
    )(
        chosen, valence_energy, conduction_energy, valence, conduction,
        jnp.asarray(plane_high), jnp.asarray(plane_low), jnp.asarray(first),
    )


DEPTH = 256


def plane_codes(point):
    first = point // (NR2 * NR3)
    second = point // NR3 % NR2
    third = point % NR3
    mirrored = third >= HALF
    first = jnp.where(mirrored, (NR1 - first) % NR1, first)
    second = jnp.where(mirrored, (NR2 - second) % NR2, second)
    third = jnp.where(mirrored, NR3 - third, third)
    column = second % 2 * PER_PARITY + second // 2 * HALF + third
    sign = jnp.where(mirrored, -1.0, 1.0)
    return column, first, sign


def pick_strip(point, table):
    width = point.shape[1]
    column, first, sign = plane_codes(point)
    counter = lax.broadcasted_iota(jnp.int32, (DEPTH, width), 0)
    counter = counter.astype(jnp.float32).astype(jnp.bfloat16)
    total = None
    for part in range(COLUMNS // DEPTH):
        wanted = (column - part * DEPTH).astype(jnp.float32).astype(jnp.bfloat16)
        hot = jnp.where(counter == wanted, jnp.bfloat16(1), jnp.bfloat16(0))
        term = dot32(table[:, part * DEPTH : (part + 1) * DEPTH], hot)
        total = term if total is None else total + term
    chosen = lax.broadcasted_iota(jnp.int32, (NR1, width), 0) == first
    rows = []
    for field in range(table.shape[0] // NR1):
        block = jnp.where(chosen, total[field * NR1 : (field + 1) * NR1, :], 0.0)
        row = jnp.sum(block, axis=0, keepdims=True)
        rows.append(row * sign if field % 2 else row)
    return jnp.concatenate(rows, axis=0).astype(jnp.bfloat16)


def pick_cost(table, waves):
    return pl.CostEstimate(
        flops=2 * table.size * waves, bytes_accessed=table.size * 2 + waves * 32, transcendentals=0
    )


def pick(strips, table, at, turn, together, steps):
    width = strips.shape[3]
    fields = table.shape[0] // NR1
    each = together * width

    def kernel(_, points, table, picked):
        point = jnp.concatenate([points[device, 0] for device in range(together)], axis=1)
        picked[...] = pick_strip(point, table)

    return pl.pallas_call(
        kernel,
        grid_spec=pltpu.PrefetchScalarGridSpec(
            num_scalar_prefetch=1,
            grid=(steps,),
            in_specs=[
                pl.BlockSpec((together, 1, 1, width), lambda i, at: (at[0] + i, turn, 0, 0)),
                pl.BlockSpec(memory_space=pltpu.VMEM),
            ],
            out_specs=pl.BlockSpec((fields, each), lambda i, at: (0, i)),
        ),
        out_shape=jax.ShapeDtypeStruct((fields, steps * each), jnp.bfloat16),
        compiler_params=pltpu.CompilerParams(vmem_limit_bytes=VMEM // 3),
        cost_estimate=pick_cost(table, steps * each),
        name="pick",
    )(at, strips, table)


def pick_columns(strips, table, me, devices):
    width = strips.shape[3]
    fields = table.shape[0] // NR1
    per_group = devices // 2

    def kernel(me, points, table, mine, other, first, second):
        values = pick_strip(jnp.concatenate([points[0, 0], points[0, 1]], axis=1), table)
        first[...] = values[:, :width]
        second[...] = values[:, width:]
        is_mine = pl.program_id(0) // per_group == me[0]

        @pl.when(is_mine)
        def _():
            mine[...] = values

        @pl.when(jnp.logical_not(is_mine))
        def _():
            other[...] = values

    def of_group(i, group):
        return (0, jnp.clip(i - group * per_group, 0, per_group - 1))

    return pl.pallas_call(
        kernel,
        grid_spec=pltpu.PrefetchScalarGridSpec(
            num_scalar_prefetch=1,
            grid=(devices,),
            in_specs=[
                pl.BlockSpec((1, 2, 1, width), lambda i, me: (i, 0, 0, 0)),
                pl.BlockSpec(memory_space=pltpu.VMEM),
            ],
            out_specs=[
                pl.BlockSpec((fields, 2 * width), lambda i, me: of_group(i, me[0])),
                pl.BlockSpec((fields, 2 * width), lambda i, me: of_group(i, 1 - me[0])),
                pl.BlockSpec((fields, width), lambda i, me: (0, i)),
                pl.BlockSpec((fields, width), lambda i, me: (0, i)),
            ],
        ),
        out_shape=[jax.ShapeDtypeStruct((fields, devices * width), jnp.bfloat16)] * 4,
        compiler_params=pltpu.CompilerParams(vmem_limit_bytes=VMEM // 3),
        cost_estimate=pick_cost(table, 2 * devices * width),
        name="pick_columns",
    )(me, strips, table)


def response_kernel(pieces, scale, place, *refs):
    out, left, right = refs[-3:]
    rows, refs = refs[: -3 - len(pieces)], refs[-3 - len(pieces) : -3]

    @pl.when(pl.program_id(0) == 0)
    def _():
        if len(rows) == 1:
            left[...] = rows[0][...].T
        else:
            count = rows[0].shape[1]
            parts = [part[...].astype(jnp.float32).reshape(-1, 1, 8, count) for part in rows]
            left[...] = jnp.concatenate(parts, axis=1).reshape(-1, count).T.astype(jnp.bfloat16)

    for offsets, block in zip(pieces, refs):
        size = block.shape[0] // len(offsets)
        for position, offset in enumerate(offsets):
            start = pl.multiple_of(jnp.bitwise_xor(place[0], offset) * size, size)
            right[pl.ds(start, size), :] = block[position * size : (position + 1) * size, :]

    out[...] = dot32(left[...], right[...]) * scale


def response(out, shape, row_block, first, steps, place, rows, pieces, blocks, scale, width):
    depth, count = sum(part.shape[0] for part in rows), rows[0].shape[1]

    def kernel(place, *refs):
        refs = refs[: len(rows) + len(blocks)] + refs[-3:]
        response_kernel(pieces, scale, place, *refs)

    operands = [place, *rows, *blocks]
    in_specs = [pl.BlockSpec(memory_space=pltpu.SMEM)] + [whole(part) for part in rows]
    in_specs += [pl.BlockSpec((block.shape[0], width), lambda i: (0, first + i)) for block in blocks]
    aliases = {}
    if out is not None:
        aliases = {len(operands): 0}
        operands.append(out)
        in_specs.append(pl.BlockSpec(memory_space=pl.ANY))
    return pl.pallas_call(
        kernel,
        grid=(steps,),
        in_specs=in_specs,
        out_specs=pl.BlockSpec((count, width), lambda i: (row_block, first + i)),
        out_shape=jax.ShapeDtypeStruct(shape, jnp.float32),
        scratch_shapes=[
            pltpu.VMEM((count, depth), jnp.bfloat16),
            pltpu.VMEM((depth, width), jnp.bfloat16),
        ],
        input_output_aliases=aliases,
        compiler_params=pltpu.CompilerParams(vmem_limit_bytes=VMEM // 2),
        cost_estimate=pl.CostEstimate(
            flops=2 * depth * count * steps * width,
            bytes_accessed=4 * count * steps * width,
            transcendentals=0,
        ),
        name="response",
    )(*operands)


def after(values, *others):
    return lax.optimization_barrier((values, others))[0]


def any_mesh(groups, size, table, grid_map, depth, scale):
    zero = jnp.zeros((1,), jnp.int32)
    strips = grid_map.reshape(-1, 1, 1, 1024)
    everything = pick(strips, table, zero, 0, 1, strips.shape[0])
    fields = everything.shape[0]
    block = lax.all_to_all(everything[:, :NGC], "grp", split_axis=1, concat_axis=0, tiled=True)
    blocks = lax.all_gather(block, "dev", axis=0, tiled=True)
    here = lax.all_to_all(everything, "dev", split_axis=1, concat_axis=0, tiled=True)
    rows = lax.all_gather(here, "grp", axis=0).reshape(groups, size, fields, -1)
    rows = rows.transpose(1, 0, 2, 3).reshape(depth, -1)
    shape = (rows.shape[1], NGC // groups)
    steps = shape[1] // 512
    return response(None, shape, 0, 0, steps, zero, [rows], [tuple(range(size))], [blocks], scale, 512)


def per_device(
    groups, size, valence_orbitals, conduction_orbitals, valence_energy, conduction_energy, pair_index, grid_map
):
    own_rows = grid_map.shape[0] // size
    fields = 2 * pair_index.shape[1]
    depth = groups * size * fields
    scale = -1.0 / math.sqrt(depth // 2)
    table = spectra_table(
        valence_orbitals, conduction_orbitals, valence_energy, conduction_energy, pair_index
    )
    if groups != 2 or size != 16:
        return any_mesh(groups, size, table, grid_map, depth, scale)

    me = lax.axis_index("grp")
    place = jnp.full((1,), lax.axis_index("dev"), jnp.int32)
    half = own_rows // 2
    strips = grid_map.reshape(size, 2, 1, half)
    def across(values):
        return lax.ppermute(values, "grp", [(0, 1), (1, 0)])

    def swap(values, bit):
        return lax.ppermute(values, "dev", [(i, i ^ bit) for i in range(size)])

    def stack(*values):
        return jnp.concatenate(values, axis=0)

    def high(turn, first, count, *others):
        at = jnp.full((1,), first // 2, jnp.int32)
        return pick(strips, table, after(at, *others), turn, 2, count // 2)

    def to_rows(*values):
        values = jnp.concatenate(values, axis=1)
        return lax.all_to_all(values, "dev", split_axis=1, concat_axis=0, tiled=True)

    middle, quarter = size // 2, size // 4
    mine, other, *columns = pick_columns(strips, table, jnp.full((1,), me, jnp.int32), middle)
    sent = across(other)
    rest0 = [high(0, middle, quarter, mine)]
    own = stack(mine, after(sent, *rest0))
    held = {offset: swap(own, offset) for offset in (8, 4, 2)}
    rest0.append(high(0, middle + quarter, quarter, own))
    here0 = to_rows(columns[0], *rest0)
    held, rest0 = lax.optimization_barrier((held, rest0))
    held[12], held[10], held[6] = swap(held[8], 4), swap(held[8], 2), swap(held[4], 2)
    rest1 = [high(1, middle, quarter, *rest0)]
    held[14] = swap(held[12], 2)
    there0 = across(after(here0, *rest1))
    rest1.append(high(1, middle + quarter, quarter, here0, held[12], held[10], held[6], *rest1))
    columns, there0 = lax.optimization_barrier((columns, there0))
    here1 = to_rows(columns[1], *rest1)
    held[0], held[14] = own, after(held[14], here1)
    held.update({offset + 1: swap(block, 1) for offset, block in list(held.items())})
    pieces = [(offset,) for offset in held]
    blocks = list(held.values())

    shape = (own_rows, NGC // groups)
    there1 = across(here1)
    out = None
    for turn, rows in enumerate(([here0, there0], [here1, there1])):
        out = response(out, shape, turn, 0, shape[1] // own_rows, place, rows, pieces, blocks, scale, own_rows)
    return out


def solution(mesh):
    groups, size = mesh.shape["grp"], mesh.shape["dev"]

    def body(*args):
        return per_device(groups, size, *args)

    in_specs = (P(), P("dev", None, None), P(), P("dev"), P("dev", "grp"), P())
    out_specs = P("dev", "grp")
    return jax.shard_map(body, mesh=mesh, in_specs=in_specs, out_specs=out_specs, check_vma=False)
```

```python
import math

import jax
import jax.numpy as jnp
import numpy as np
from jax import lax
from jax.experimental import pallas as pl
from jax.experimental.pallas import tpu as pltpu
from jax.sharding import PartitionSpec as P

NR1 = 48
NR2 = 48
NR3 = 48
NGC = 12288
HALF = NR3 // 2 + 1
FOLD = NR2 * NR3 // 2
LANES = 128
PER_PARITY = -(-(NR2 // 2 * HALF) // LANES) * LANES
COLUMNS = 2 * PER_PARITY
VMEM = 60 * 1024 * 1024
SPECTRA_VMEM = 60 * 1024 * 1024


def split_bf16(values):
    high = values.astype(jnp.bfloat16)
    low = (values - high.astype(values.dtype)).astype(jnp.bfloat16)
    return high, low


def plane_tables():
    r2 = np.arange(NR2 // 2)[:, None]
    r3 = np.arange(NR3)[None, :]
    table = np.zeros((2, FOLD, PER_PARITY, 2))
    for parity in range(2):
        for half_k2 in range(NR2 // 2):
            k2 = 2 * half_k2 + parity
            for k3 in range(HALF):
                angle = 2 * np.pi * ((k2 * r2 * NR3 + k3 * r3 * NR2) % (NR2 * NR3)) / (NR2 * NR3)
                table[parity, :, half_k2 * HALF + k3, 0] = np.cos(angle).reshape(-1)
                table[parity, :, half_k2 * HALF + k3, 1] = np.sin(angle).reshape(-1)
    table = table.transpose(0, 1, 3, 2).reshape(2, FOLD, 2 * PER_PARITY).astype(np.float32)
    high = table.astype(jnp.bfloat16)
    low = (table - high.astype(np.float32)).astype(jnp.bfloat16)
    return np.stack([high[0], low[0], high[1], low[1]])


def first_tables():
    counter = np.arange(NR1)
    angle = 2 * np.pi * (counter[:, None] * counter[None, :] % NR1) / NR1
    cosine, sine = np.cos(angle), np.sin(angle)
    table = np.block([[cosine, -sine], [-sine, -cosine]]).astype(np.float32)
    high = table.astype(jnp.bfloat16)
    low = (table - high.astype(np.float32)).astype(jnp.bfloat16)
    return np.concatenate([high, low])


def dot32(left, right):
    return jnp.dot(left, right, preferred_element_type=jnp.float32)


def three_products(high_low, right_high, right_low):
    half = high_low.shape[0] // 2
    both = dot32(high_low, right_high)
    return both[:half] + (both[half:] + dot32(high_low[:half], right_low))


def spectrum_kernel(
    pairs, chosen, valence_energy, conduction_energy, valence, conduction,
    plane_table, first, table, folded, plane,
):
    step = pl.program_id(0)
    rows = pairs * NR1
    bands_here = conduction.shape[0]

    @pl.when(step == 0)
    def _():
        for pair in range(pairs):
            left = valence[chosen[0, pair] // bands_here].astype(jnp.float32)
            right = conduction[chosen[0, pair] % bands_here].astype(jnp.float32)
            density = left * right
            for parity in range(2):
                if parity == 0:
                    values = density[:, :FOLD] + density[:, FOLD:]
                else:
                    values = density[:, :FOLD] - density[:, FOLD:]
                high, low = split_bf16(values)
                folded[parity, pair * NR1 : (pair + 1) * NR1, :] = high
                folded[parity, rows + pair * NR1 : rows + (pair + 1) * NR1, :] = low

    @pl.when(step % 2 == 0)
    def _():
        both = dot32(folded[step // 2], plane_table[0])
        plane[...] = both[:rows] + both[rows:]

    @pl.when(step % 2 == 1)
    def _():
        total = plane[...] + dot32(folded[step // 2, :rows], plane_table[0])
        stacked = jnp.concatenate(
            [
                jnp.concatenate(
                    [
                        total[pair * NR1 : (pair + 1) * NR1, :PER_PARITY],
                        total[pair * NR1 : (pair + 1) * NR1, PER_PARITY:],
                    ],
                    axis=0,
                )
                for pair in range(pairs)
            ],
            axis=1,
        )
        spectra = three_products(first[...], *split_bf16(stacked))
        inverse_root = 1.0 / math.sqrt(NR1 * NR2 * NR3)
        for pair in range(pairs):
            gap = conduction_energy[chosen[0, pair] % bands_here] - valence_energy[chosen[0, pair] // bands_here]
            factor = jnp.sqrt(4.0 / jnp.full((8, LANES), gap, jnp.float32)) * inverse_root
            block = spectra[:, pair * PER_PARITY : (pair + 1) * PER_PARITY]
            block = block * factor[0:1, 0:1]
            table[pair * 2 * NR1 : (pair + 1) * 2 * NR1, :] = block.astype(jnp.bfloat16)


def whole(array):
    return pl.BlockSpec(array.shape, lambda *_: (0,) * array.ndim)


def spectra_table(valence, conduction, valence_energy, conduction_energy, chosen):
    pairs = chosen.shape[1]
    plane_table = plane_tables()
    first = first_tables()
    scalars = pl.BlockSpec(memory_space=pltpu.SMEM)
    tile = pl.BlockSpec((1, FOLD, 2 * PER_PARITY), lambda i: (i, 0, 0))

    def kernel(*refs):
        spectrum_kernel(pairs, *refs)

    return pl.pallas_call(
        kernel,
        grid=(4,),
        in_specs=[scalars, scalars, scalars, whole(valence), whole(conduction), tile]
        + [whole(first)],
        out_specs=pl.BlockSpec((pairs * 2 * NR1, PER_PARITY), lambda i: (0, i // 2)),
        out_shape=jax.ShapeDtypeStruct((pairs * 2 * NR1, COLUMNS), jnp.bfloat16),
        scratch_shapes=[
            pltpu.VMEM((2, 2 * pairs * NR1, FOLD), jnp.bfloat16),
            pltpu.VMEM((pairs * NR1, 2 * PER_PARITY), jnp.float32),
        ],
        compiler_params=pltpu.CompilerParams(vmem_limit_bytes=SPECTRA_VMEM),
        name="spectra",
    )(
        chosen, valence_energy, conduction_energy, valence, conduction,
        jnp.asarray(plane_table), jnp.asarray(first),
    )


DEPTH = 256


def plane_codes(point):
    first = point // (NR2 * NR3)
    second = point // NR3 % NR2
    third = point % NR3
    mirrored = third >= HALF
    first = jnp.where(mirrored, (NR1 - first) % NR1, first)
    second = jnp.where(mirrored, (NR2 - second) % NR2, second)
    third = jnp.where(mirrored, NR3 - third, third)
    column = second % 2 * PER_PARITY + second // 2 * HALF + third
    sign = jnp.where(mirrored, -1.0, 1.0)
    return column, first, sign


def pick_strip(point, table):
    width = point.shape[1]
    column, first, sign = plane_codes(point)
    counter = lax.broadcasted_iota(jnp.int32, (DEPTH, width), 0)
    counter = counter.astype(jnp.float32).astype(jnp.bfloat16)
    total = None
    for part in range(COLUMNS // DEPTH):
        wanted = (column - part * DEPTH).astype(jnp.float32).astype(jnp.bfloat16)
        hot = jnp.where(counter == wanted, jnp.bfloat16(1), jnp.bfloat16(0))
        term = dot32(table[:, part * DEPTH : (part + 1) * DEPTH], hot)
        total = term if total is None else total + term
    chosen = lax.broadcasted_iota(jnp.int32, (NR1, width), 0) == first
    rows = []
    for field in range(table.shape[0] // NR1):
        block = jnp.where(chosen, total[field * NR1 : (field + 1) * NR1, :], 0.0)
        row = jnp.sum(block, axis=0, keepdims=True)
        rows.append(row * sign if field % 2 else row)
    return jnp.concatenate(rows, axis=0).astype(jnp.bfloat16)


def pick_cost(table, waves):
    return pl.CostEstimate(
        flops=2 * table.size * waves, bytes_accessed=table.size * 2 + waves * 32, transcendentals=0
    )


def pick(strips, table, at, turn, together, steps):
    width = strips.shape[3]
    fields = table.shape[0] // NR1
    each = together * width

    def kernel(_, points, table, picked):
        point = jnp.concatenate([points[device, 0] for device in range(together)], axis=1)
        picked[...] = pick_strip(point, table)

    return pl.pallas_call(
        kernel,
        grid_spec=pltpu.PrefetchScalarGridSpec(
            num_scalar_prefetch=1,
            grid=(steps,),
            in_specs=[
                pl.BlockSpec((together, 1, 1, width), lambda i, at: (at[0] + i, turn, 0, 0)),
                pl.BlockSpec(memory_space=pltpu.VMEM),
            ],
            out_specs=pl.BlockSpec((fields, each), lambda i, at: (0, i)),
        ),
        out_shape=jax.ShapeDtypeStruct((fields, steps * each), jnp.bfloat16),
        compiler_params=pltpu.CompilerParams(vmem_limit_bytes=VMEM // 3),
        cost_estimate=pick_cost(table, steps * each),
        name="pick",
    )(at, strips, table)


def pick_columns(strips, table, me, devices):
    width = strips.shape[3]
    fields = table.shape[0] // NR1
    per_group = devices // 2

    def kernel(me, points, table, mine, other, first, second):
        values = pick_strip(jnp.concatenate([points[0, 0], points[0, 1]], axis=1), table)
        first[...] = values[:, :width]
        second[...] = values[:, width:]
        is_mine = pl.program_id(0) // per_group == me[0]

        @pl.when(is_mine)
        def _():
            mine[...] = values

        @pl.when(jnp.logical_not(is_mine))
        def _():
            other[...] = values

    def of_group(i, group):
        return (0, jnp.clip(i - group * per_group, 0, per_group - 1))

    return pl.pallas_call(
        kernel,
        grid_spec=pltpu.PrefetchScalarGridSpec(
            num_scalar_prefetch=1,
            grid=(devices,),
            in_specs=[
                pl.BlockSpec((1, 2, 1, width), lambda i, me: (i, 0, 0, 0)),
                pl.BlockSpec(memory_space=pltpu.VMEM),
            ],
            out_specs=[
                pl.BlockSpec((fields, 2 * width), lambda i, me: of_group(i, me[0])),
                pl.BlockSpec((fields, 2 * width), lambda i, me: of_group(i, 1 - me[0])),
                pl.BlockSpec((fields, width), lambda i, me: (0, i)),
                pl.BlockSpec((fields, width), lambda i, me: (0, i)),
            ],
        ),
        out_shape=[jax.ShapeDtypeStruct((fields, devices * width), jnp.bfloat16)] * 4,
        compiler_params=pltpu.CompilerParams(vmem_limit_bytes=VMEM // 3),
        cost_estimate=pick_cost(table, 2 * devices * width),
        name="pick_columns",
    )(me, strips, table)


def response_kernel(pieces, scale, place, *refs):
    out, left, right = refs[-3:]
    rows, refs = refs[: -3 - len(pieces)], refs[-3 - len(pieces) : -3]

    @pl.when(pl.program_id(0) == 0)
    def _():
        if len(rows) == 1:
            left[...] = rows[0][...].T
        else:
            count = rows[0].shape[1]
            parts = [part[...].astype(jnp.float32).reshape(-1, 1, 8, count) for part in rows]
            left[...] = jnp.concatenate(parts, axis=1).reshape(-1, count).T.astype(jnp.bfloat16)

    for offsets, block in zip(pieces, refs):
        size = block.shape[0] // len(offsets)
        for position, offset in enumerate(offsets):
            start = pl.multiple_of(jnp.bitwise_xor(place[0], offset) * size, size)
            right[pl.ds(start, size), :] = block[position * size : (position + 1) * size, :]

    out[...] = dot32(left[...], right[...]) * scale


def response(out, shape, row_block, first, steps, place, rows, pieces, blocks, scale, width):
    depth, count = sum(part.shape[0] for part in rows), rows[0].shape[1]

    def kernel(place, *refs):
        refs = refs[: len(rows) + len(blocks)] + refs[-3:]
        response_kernel(pieces, scale, place, *refs)

    operands = [place, *rows, *blocks]
    in_specs = [pl.BlockSpec(memory_space=pltpu.SMEM)] + [whole(part) for part in rows]
    in_specs += [pl.BlockSpec((block.shape[0], width), lambda i: (0, first + i)) for block in blocks]
    aliases = {}
    if out is not None:
        aliases = {len(operands): 0}
        operands.append(out)
        in_specs.append(pl.BlockSpec(memory_space=pl.ANY))
    return pl.pallas_call(
        kernel,
        grid=(steps,),
        in_specs=in_specs,
        out_specs=pl.BlockSpec((count, width), lambda i: (row_block, first + i)),
        out_shape=jax.ShapeDtypeStruct(shape, jnp.float32),
        scratch_shapes=[
            pltpu.VMEM((count, depth), jnp.bfloat16),
            pltpu.VMEM((depth, width), jnp.bfloat16),
        ],
        input_output_aliases=aliases,
        compiler_params=pltpu.CompilerParams(vmem_limit_bytes=VMEM // 2),
        cost_estimate=pl.CostEstimate(
            flops=2 * depth * count * steps * width,
            bytes_accessed=4 * count * steps * width,
            transcendentals=0,
        ),
        name="response",
    )(*operands)


def after(values, *others):
    return lax.optimization_barrier((values, others))[0]


def any_mesh(groups, size, table, grid_map, depth, scale):
    zero = jnp.zeros((1,), jnp.int32)
    strips = grid_map.reshape(-1, 1, 1, 1024)
    everything = pick(strips, table, zero, 0, 1, strips.shape[0])
    fields = everything.shape[0]
    block = lax.all_to_all(everything[:, :NGC], "grp", split_axis=1, concat_axis=0, tiled=True)
    blocks = lax.all_gather(block, "dev", axis=0, tiled=True)
    here = lax.all_to_all(everything, "dev", split_axis=1, concat_axis=0, tiled=True)
    rows = lax.all_gather(here, "grp", axis=0).reshape(groups, size, fields, -1)
    rows = rows.transpose(1, 0, 2, 3).reshape(depth, -1)
    shape = (rows.shape[1], NGC // groups)
    steps = shape[1] // 512
    return response(None, shape, 0, 0, steps, zero, [rows], [tuple(range(size))], [blocks], scale, 512)


def per_device(
    groups, size, valence_orbitals, conduction_orbitals, valence_energy, conduction_energy, pair_index, grid_map
):
    own_rows = grid_map.shape[0] // size
    fields = 2 * pair_index.shape[1]
    depth = groups * size * fields
    scale = -1.0 / math.sqrt(depth // 2)
    table = spectra_table(
        valence_orbitals, conduction_orbitals, valence_energy, conduction_energy, pair_index
    )
    if groups != 2 or size != 16:
        return any_mesh(groups, size, table, grid_map, depth, scale)

    me = lax.axis_index("grp")
    place = jnp.full((1,), lax.axis_index("dev"), jnp.int32)
    half = own_rows // 2
    strips = grid_map.reshape(size, 2, 1, half)
    def across(values):
        return lax.ppermute(values, "grp", [(0, 1), (1, 0)])

    def swap(values, bit):
        return lax.ppermute(values, "dev", [(i, i ^ bit) for i in range(size)])

    def stack(*values):
        return jnp.concatenate(values, axis=0)

    def high(turn, first, count, *others):
        at = jnp.full((1,), first // 2, jnp.int32)
        return pick(strips, table, after(at, *others), turn, 2, count // 2)

    def to_rows(*values):
        values = jnp.concatenate(values, axis=1)
        return lax.all_to_all(values, "dev", split_axis=1, concat_axis=0, tiled=True)

    middle, quarter = size // 2, size // 4
    mine, other, *columns = pick_columns(strips, table, jnp.full((1,), me, jnp.int32), middle)
    sent = across(other)
    rest0 = [high(0, middle, quarter, mine)]
    own = stack(mine, after(sent, *rest0))
    held = {offset: swap(own, offset) for offset in (8, 4, 2)}
    rest0.append(high(0, middle + quarter, quarter, own))
    here0 = to_rows(columns[0], *rest0)
    held, rest0 = lax.optimization_barrier((held, rest0))
    held[12], held[10], held[6] = swap(held[8], 4), swap(held[8], 2), swap(held[4], 2)
    rest1 = [high(1, middle, quarter, *rest0)]
    held[14] = swap(held[12], 2)
    there0 = across(after(here0, *rest1))
    rest1.append(high(1, middle + quarter, quarter, here0, held[12], held[10], held[6], *rest1))
    columns, there0 = lax.optimization_barrier((columns, there0))
    here1 = to_rows(columns[1], *rest1)
    held[0], held[14] = own, after(held[14], here1)
    held.update({offset + 1: swap(block, 1) for offset, block in list(held.items())})
    pieces = [(offset,) for offset in held]
    blocks = list(held.values())

    shape = (own_rows, NGC // groups)
    there1 = across(here1)
    out = None
    for turn, rows in enumerate(([here0, there0], [here1, there1])):
        out = response(out, shape, turn, 0, shape[1] // own_rows, place, rows, pieces, blocks, scale, own_rows)
    return out


def solution(mesh):
    groups, size = mesh.shape["grp"], mesh.shape["dev"]

    def body(*args):
        return per_device(groups, size, *args)

    in_specs = (P(), P("dev", None, None), P(), P("dev"), P("dev", "grp"), P())
    out_specs = P("dev", "grp")
    return jax.shard_map(body, mesh=mesh, in_specs=in_specs, out_specs=out_specs, check_vma=False)
```

```python
import math

import jax
import jax.numpy as jnp
import numpy as np
from jax import lax
from jax.experimental import pallas as pl
from jax.experimental.pallas import tpu as pltpu
from jax.sharding import PartitionSpec as P

NR1 = 48
NR2 = 48
NR3 = 48
NGC = 12288
HALF = NR3 // 2 + 1
FOLD = NR2 * NR3 // 2
LANES = 128
PER_PARITY = -(-(NR2 // 2 * HALF) // LANES) * LANES
COLUMNS = 2 * PER_PARITY
VMEM = 60 * 1024 * 1024
SPECTRA_VMEM = 60 * 1024 * 1024


def split_bf16(values):
    high = values.astype(jnp.bfloat16)
    low = (values - high.astype(values.dtype)).astype(jnp.bfloat16)
    return high, low


def plane_tables():
    r2 = np.arange(NR2 // 2)[:, None]
    r3 = np.arange(NR3)[None, :]
    table = np.zeros((2, FOLD, PER_PARITY, 2))
    for parity in range(2):
        for half_k2 in range(NR2 // 2):
            k2 = 2 * half_k2 + parity
            for k3 in range(HALF):
                angle = 2 * np.pi * ((k2 * r2 * NR3 + k3 * r3 * NR2) % (NR2 * NR3)) / (NR2 * NR3)
                table[parity, :, half_k2 * HALF + k3, 0] = np.cos(angle).reshape(-1)
                table[parity, :, half_k2 * HALF + k3, 1] = np.sin(angle).reshape(-1)
    table = table.transpose(0, 1, 3, 2).reshape(2, FOLD, 2 * PER_PARITY).astype(np.float32)
    high = table.astype(jnp.bfloat16)
    low = (table - high.astype(np.float32)).astype(jnp.bfloat16)
    return np.stack([high[0], low[0], high[1], low[1]])


def first_tables():
    counter = np.arange(NR1)
    angle = 2 * np.pi * (counter[:, None] * counter[None, :] % NR1) / NR1
    cosine, sine = np.cos(angle), np.sin(angle)
    table = np.block([[cosine, -sine], [-sine, -cosine]]).astype(np.float32)
    high = table.astype(jnp.bfloat16)
    low = (table - high.astype(np.float32)).astype(jnp.bfloat16)
    return np.concatenate([high, low])


def dot32(left, right):
    return jnp.dot(left, right, preferred_element_type=jnp.float32)


def three_products(high_low, right_high, right_low):
    half = high_low.shape[0] // 2
    both = dot32(high_low, right_high)
    return both[:half] + (both[half:] + dot32(high_low[:half], right_low))


def spectrum_kernel(
    pairs, chosen, valence_energy, conduction_energy, valence, conduction,
    plane_table, first, table, folded, plane,
):
    step = pl.program_id(0)
    rows = pairs * NR1
    bands_here = conduction.shape[0]

    @pl.when(step == 0)
    def _():
        for pair in range(pairs):
            left = valence[chosen[0, pair] // bands_here].astype(jnp.float32)
            right = conduction[chosen[0, pair] % bands_here].astype(jnp.float32)
            density = left * right
            for parity in range(2):
                if parity == 0:
                    values = density[:, :FOLD] + density[:, FOLD:]
                else:
                    values = density[:, :FOLD] - density[:, FOLD:]
                high, low = split_bf16(values)
                folded[parity, pair * NR1 : (pair + 1) * NR1, :] = high
                folded[parity, rows + pair * NR1 : rows + (pair + 1) * NR1, :] = low

    @pl.when(step % 2 == 0)
    def _():
        both = dot32(folded[step // 2], plane_table[0])
        plane[...] = both[:rows] + both[rows:]

    @pl.when(step % 2 == 1)
    def _():
        total = plane[...] + dot32(folded[step // 2, :rows], plane_table[0])
        stacked = jnp.concatenate(
            [
                jnp.concatenate(
                    [
                        total[pair * NR1 : (pair + 1) * NR1, :PER_PARITY],
                        total[pair * NR1 : (pair + 1) * NR1, PER_PARITY:],
                    ],
                    axis=0,
                )
                for pair in range(pairs)
            ],
            axis=1,
        )
        spectra = three_products(first[...], *split_bf16(stacked))
        inverse_root = 1.0 / math.sqrt(NR1 * NR2 * NR3)
        for pair in range(pairs):
            gap = conduction_energy[chosen[0, pair] % bands_here] - valence_energy[chosen[0, pair] // bands_here]
            factor = jnp.sqrt(4.0 / jnp.full((8, LANES), gap, jnp.float32)) * inverse_root
            block = spectra[:, pair * PER_PARITY : (pair + 1) * PER_PARITY]
            block = block * factor[0:1, 0:1]
            table[pair * 2 * NR1 : (pair + 1) * 2 * NR1, :] = block.astype(jnp.bfloat16)


def whole(array):
    return pl.BlockSpec(array.shape, lambda *_: (0,) * array.ndim)


def spectra_table(valence, conduction, valence_energy, conduction_energy, chosen):
    pairs = chosen.shape[1]
    plane_table = plane_tables()
    first = first_tables()
    scalars = pl.BlockSpec(memory_space=pltpu.SMEM)
    tile = pl.BlockSpec((1, FOLD, 2 * PER_PARITY), lambda i: (i, 0, 0))

    def kernel(*refs):
        spectrum_kernel(pairs, *refs)

    return pl.pallas_call(
        kernel,
        grid=(4,),
        in_specs=[scalars, scalars, scalars, whole(valence), whole(conduction), tile]
        + [whole(first)],
        out_specs=pl.BlockSpec((pairs * 2 * NR1, PER_PARITY), lambda i: (0, i // 2)),
        out_shape=jax.ShapeDtypeStruct((pairs * 2 * NR1, COLUMNS), jnp.bfloat16),
        scratch_shapes=[
            pltpu.VMEM((2, 2 * pairs * NR1, FOLD), jnp.bfloat16),
            pltpu.VMEM((pairs * NR1, 2 * PER_PARITY), jnp.float32),
        ],
        compiler_params=pltpu.CompilerParams(vmem_limit_bytes=SPECTRA_VMEM),
        name="spectra",
    )(
        chosen, valence_energy, conduction_energy, valence, conduction,
        jnp.asarray(plane_table), jnp.asarray(first),
    )


DEPTH = 256


def plane_codes(point):
    first = point // (NR2 * NR3)
    second = point // NR3 % NR2
    third = point % NR3
    mirrored = third >= HALF
    first = jnp.where(mirrored, (NR1 - first) % NR1, first)
    second = jnp.where(mirrored, (NR2 - second) % NR2, second)
    third = jnp.where(mirrored, NR3 - third, third)
    column = second % 2 * PER_PARITY + second // 2 * HALF + third
    sign = jnp.where(mirrored, -1.0, 1.0)
    return column, first, sign


def pick_strip(point, table):
    width = point.shape[1]
    column, first, sign = plane_codes(point)
    counter = lax.broadcasted_iota(jnp.int32, (DEPTH, width), 0)
    counter = counter.astype(jnp.float32).astype(jnp.bfloat16)
    total = None
    for part in range(COLUMNS // DEPTH):
        wanted = (column - part * DEPTH).astype(jnp.float32).astype(jnp.bfloat16)
        hot = jnp.where(counter == wanted, jnp.bfloat16(1), jnp.bfloat16(0))
        term = dot32(table[:, part * DEPTH : (part + 1) * DEPTH], hot)
        total = term if total is None else total + term
    chosen = lax.broadcasted_iota(jnp.int32, (NR1, width), 0) == first
    rows = []
    for field in range(table.shape[0] // NR1):
        block = jnp.where(chosen, total[field * NR1 : (field + 1) * NR1, :], 0.0)
        row = jnp.sum(block, axis=0, keepdims=True)
        rows.append(row * sign if field % 2 else row)
    return jnp.concatenate(rows, axis=0).astype(jnp.bfloat16)


def pick_cost(table, waves):
    return pl.CostEstimate(
        flops=2 * table.size * waves, bytes_accessed=table.size * 2 + waves * 32, transcendentals=0
    )


def pick(strips, table, at, turn, together, steps):
    width = strips.shape[3]
    fields = table.shape[0] // NR1
    each = together * width

    def kernel(_, points, table, picked):
        point = jnp.concatenate([points[device, 0] for device in range(together)], axis=1)
        picked[...] = pick_strip(point, table)

    return pl.pallas_call(
        kernel,
        grid_spec=pltpu.PrefetchScalarGridSpec(
            num_scalar_prefetch=1,
            grid=(steps,),
            in_specs=[
                pl.BlockSpec((together, 1, 1, width), lambda i, at: (at[0] + i, turn, 0, 0)),
                pl.BlockSpec(memory_space=pltpu.VMEM),
            ],
            out_specs=pl.BlockSpec((fields, each), lambda i, at: (0, i)),
        ),
        out_shape=jax.ShapeDtypeStruct((fields, steps * each), jnp.bfloat16),
        compiler_params=pltpu.CompilerParams(vmem_limit_bytes=VMEM // 3),
        cost_estimate=pick_cost(table, steps * each),
        name="pick",
    )(at, strips, table)


def pick_columns(strips, table, me, devices):
    width = strips.shape[3]
    fields = table.shape[0] // NR1
    per_group = devices // 2

    def kernel(me, points, table, mine, other, first, second):
        values = pick_strip(jnp.concatenate([points[0, 0], points[0, 1]], axis=1), table)
        first[...] = values[:, :width]
        second[...] = values[:, width:]
        is_mine = pl.program_id(0) // per_group == me[0]

        @pl.when(is_mine)
        def _():
            mine[...] = values

        @pl.when(jnp.logical_not(is_mine))
        def _():
            other[...] = values

    def of_group(i, group):
        return (0, jnp.clip(i - group * per_group, 0, per_group - 1))

    return pl.pallas_call(
        kernel,
        grid_spec=pltpu.PrefetchScalarGridSpec(
            num_scalar_prefetch=1,
            grid=(devices,),
            in_specs=[
                pl.BlockSpec((1, 2, 1, width), lambda i, me: (i, 0, 0, 0)),
                pl.BlockSpec(memory_space=pltpu.VMEM),
            ],
            out_specs=[
                pl.BlockSpec((fields, 2 * width), lambda i, me: of_group(i, me[0])),
                pl.BlockSpec((fields, 2 * width), lambda i, me: of_group(i, 1 - me[0])),
                pl.BlockSpec((fields, width), lambda i, me: (0, i)),
                pl.BlockSpec((fields, width), lambda i, me: (0, i)),
            ],
        ),
        out_shape=[jax.ShapeDtypeStruct((fields, devices * width), jnp.bfloat16)] * 4,
        compiler_params=pltpu.CompilerParams(vmem_limit_bytes=VMEM // 3),
        cost_estimate=pick_cost(table, 2 * devices * width),
        name="pick_columns",
    )(me, strips, table)


def response_kernel(pieces, scale, place, *refs):
    out, left, right = refs[-3:]
    rows, refs = refs[: -3 - len(pieces)], refs[-3 - len(pieces) : -3]

    @pl.when(pl.program_id(0) == 0)
    def _():
        if len(rows) == 1:
            left[...] = rows[0][...].T
        else:
            count = rows[0].shape[1]
            parts = [part[...].astype(jnp.float32).reshape(-1, 1, 8, count) for part in rows]
            left[...] = jnp.concatenate(parts, axis=1).reshape(-1, count).T.astype(jnp.bfloat16)

    for offsets, block in zip(pieces, refs):
        size = block.shape[0] // len(offsets)
        for position, offset in enumerate(offsets):
            start = pl.multiple_of(jnp.bitwise_xor(place[0], offset) * size, size)
            right[pl.ds(start, size), :] = block[position * size : (position + 1) * size, :]

    out[...] = dot32(left[...], right[...]) * scale


def response(out, shape, row_block, first, steps, place, rows, pieces, blocks, scale, width):
    depth, count = sum(part.shape[0] for part in rows), rows[0].shape[1]

    def kernel(place, *refs):
        refs = refs[: len(rows) + len(blocks)] + refs[-3:]
        response_kernel(pieces, scale, place, *refs)

    operands = [place, *rows, *blocks]
    in_specs = [pl.BlockSpec(memory_space=pltpu.SMEM)] + [whole(part) for part in rows]
    in_specs += [pl.BlockSpec((block.shape[0], width), lambda i: (0, first + i)) for block in blocks]
    aliases = {}
    if out is not None:
        aliases = {len(operands): 0}
        operands.append(out)
        in_specs.append(pl.BlockSpec(memory_space=pl.ANY))
    return pl.pallas_call(
        kernel,
        grid=(steps,),
        in_specs=in_specs,
        out_specs=pl.BlockSpec((count, width), lambda i: (row_block, first + i)),
        out_shape=jax.ShapeDtypeStruct(shape, jnp.float32),
        scratch_shapes=[
            pltpu.VMEM((count, depth), jnp.bfloat16),
            pltpu.VMEM((depth, width), jnp.bfloat16),
        ],
        input_output_aliases=aliases,
        compiler_params=pltpu.CompilerParams(vmem_limit_bytes=VMEM // 2),
        cost_estimate=pl.CostEstimate(
            flops=2 * depth * count * steps * width,
            bytes_accessed=4 * count * steps * width,
            transcendentals=0,
        ),
        name="response",
    )(*operands)


def after(values, *others):
    return lax.optimization_barrier((values, others))[0]


def any_mesh(groups, size, table, grid_map, depth, scale):
    zero = jnp.zeros((1,), jnp.int32)
    strips = grid_map.reshape(-1, 1, 1, 1024)
    everything = pick(strips, table, zero, 0, 1, strips.shape[0])
    fields = everything.shape[0]
    block = lax.all_to_all(everything[:, :NGC], "grp", split_axis=1, concat_axis=0, tiled=True)
    blocks = lax.all_gather(block, "dev", axis=0, tiled=True)
    here = lax.all_to_all(everything, "dev", split_axis=1, concat_axis=0, tiled=True)
    rows = lax.all_gather(here, "grp", axis=0).reshape(groups, size, fields, -1)
    rows = rows.transpose(1, 0, 2, 3).reshape(depth, -1)
    shape = (rows.shape[1], NGC // groups)
    steps = shape[1] // 512
    return response(None, shape, 0, 0, steps, zero, [rows], [tuple(range(size))], [blocks], scale, 512)


def per_device(
    groups, size, valence_orbitals, conduction_orbitals, valence_energy, conduction_energy, pair_index, grid_map
):
    own_rows = grid_map.shape[0] // size
    fields = 2 * pair_index.shape[1]
    depth = groups * size * fields
    scale = -1.0 / math.sqrt(depth // 2)
    table = spectra_table(
        valence_orbitals, conduction_orbitals, valence_energy, conduction_energy, pair_index
    )
    if groups != 2 or size != 16:
        return any_mesh(groups, size, table, grid_map, depth, scale)

    me = lax.axis_index("grp")
    place = jnp.full((1,), lax.axis_index("dev"), jnp.int32)
    half = own_rows // 2
    strips = grid_map.reshape(size, 2, 1, half)
    def across(values):
        return lax.ppermute(values, "grp", [(0, 1), (1, 0)])

    def swap(values, bit):
        return lax.ppermute(values, "dev", [(i, i ^ bit) for i in range(size)])

    def stack(*values):
        return jnp.concatenate(values, axis=0)

    def high(turn, first, count, *others):
        at = jnp.full((1,), first // 2, jnp.int32)
        return pick(strips, table, after(at, *others), turn, 2, count // 2)

    def to_rows(*values):
        values = jnp.concatenate(values, axis=1)
        return lax.all_to_all(values, "dev", split_axis=1, concat_axis=0, tiled=True)

    middle, quarter = size // 2, size // 4
    mine, other, *columns = pick_columns(strips, table, jnp.full((1,), me, jnp.int32), middle)
    sent = across(other)
    rest0 = [high(0, middle, quarter, mine)]
    own = stack(mine, after(sent, *rest0))
    held = {offset: swap(own, offset) for offset in (8, 4, 2)}
    rest0.append(high(0, middle + quarter, quarter, own))
    here0 = to_rows(columns[0], *rest0)
    held, rest0 = lax.optimization_barrier((held, rest0))
    held[12], held[10], held[6] = swap(held[8], 4), swap(held[8], 2), swap(held[4], 2)
    rest1 = [high(1, middle, quarter, *rest0)]
    held[14] = swap(held[12], 2)
    there0 = across(after(here0, *rest1))
    rest1.append(high(1, middle + quarter, quarter, here0, held[12], held[10], held[6], *rest1))
    columns, there0, held[14] = lax.optimization_barrier((columns, there0, held[14]))
    here1 = to_rows(columns[1], *rest1)
    held[0] = own
    held.update({offset + 1: swap(block, 1) for offset, block in list(held.items())})
    pieces = [(offset,) for offset in held]
    blocks = list(held.values())

    shape = (own_rows, NGC // groups)
    steps = shape[1] // own_rows
    rows0 = [here0, there0]
    out = response(None, shape, 0, 0, steps // 2, place, rows0, pieces, blocks, scale, own_rows)
    here1, out = lax.optimization_barrier((here1, out))
    there1 = across(here1)
    out = response(out, shape, 0, steps // 2, steps // 2, place, rows0, pieces, blocks, scale, own_rows)
    there1, out = lax.optimization_barrier((there1, out))
    return response(out, shape, 1, 0, steps, place, [here1, there1], pieces, blocks, scale, own_rows)


def solution(mesh):
    groups, size = mesh.shape["grp"], mesh.shape["dev"]

    def body(*args):
        return per_device(groups, size, *args)

    in_specs = (P(), P("dev", None, None), P(), P("dev"), P("dev", "grp"), P())
    out_specs = P("dev", "grp")
    return jax.shard_map(body, mesh=mesh, in_specs=in_specs, out_specs=out_specs, check_vma=False)
```
